32 devices in a mesh: pipe: 2 (over core), dp: 4 (over y, x), tensor: 4 (over z).
Axes of the slice: x: 2, y: 2, z: 4, core: 2. Of those that a mesh axis runs over, the one named last changes fastest.
Arguments:
- weights: bfloat16 [2, 8192, 8192], P('pipe', 'tensor', 'dp'), may hold values from -0.0625 to 0.0625
- inputs: bfloat16 [2, 2, 8, 64, 8192], P('pipe', None, 'dp', None, 'tensor'), may hold values from -150 to 150
- cotangent: bfloat16 [2, 8, 64, 8192], P(None, 'dp', None, 'tensor'), may hold values from -6 to 6
- clip_norm: float32 [1], replicated, may hold values from 8192 to 12582912
- noise: bfloat16 [2, 8192, 8192], P('pipe', 'tensor', 'dp'), may hold values from -6 to 6
Outputs:
- grads: float32 [2, 8192, 8192], P('pipe', 'tensor', 'dp')
- clip_factors: float32 [2, 8], P(None, 'dp')
The draws below stay inside these ranges and needn't reach their ends.
All inputs are finite; a program needn't handle non-finite values.
Results may differ from the reference program's by a relative error of at most 0.015.
Values may be sent and summed in bfloat16 or wider, within the bound.
A program may use at most 128 MiB of HBM per device.

```python
import math
import jax
import jax.numpy as jnp
from jax import lax

D = 8192
L = 64
MICRO = 2
SECTIONS = 2
EXAMPLES = 8
N_DP = 4


def draw_inputs(key, part):
    keys = jax.random.split(key, 3)
    base = jnp.clip(jax.random.normal(keys[0], (SECTIONS, MICRO, EXAMPLES, L, D), jnp.float32), -4.0, 4.0)
    position = jnp.arange(D, dtype=jnp.float32) / D
    trend = 0.4 * jnp.exp(math.log(6.0) * position)
    example_scale = jnp.exp(jax.random.uniform(keys[1], (1, MICRO, EXAMPLES, 1, 1), jnp.float32, 0.0, math.log(10.0)))
    rough = jnp.exp(jax.random.uniform(keys[2], (SECTIONS, 1, 1, 1, D), jnp.float32, math.log(0.6), math.log(1.6)))
    values = base * example_scale * rough * trend
    return jnp.clip(values, -150.0, 150.0).astype(jnp.bfloat16)


def draw_clip_norm(key, part):
    factor = jax.random.uniform(key, (1,), jnp.float32, 0.8, 1.2)
    return factor * (4.2 * math.sqrt(L) * D * math.sqrt(2.0 ** SECTIONS - 1.0))


def shard_levels(own_key, dims, shards, smallest, largest):
    level = 1.0
    for dim, blocks in shards:
        draws = jax.random.uniform(jax.random.fold_in(jax.random.fold_in(own_key, 6), dim), (blocks,), jnp.float32, smallest / len(shards), largest / len(shards))
        level = level * jnp.repeat(jnp.exp(draws), dims[dim] // blocks).reshape((-1,) + (1,) * (len(dims) - 1 - dim))
    return level


def scatter_about(rng, dims, spread, reach, cuts=(), kind=jnp.bfloat16):
    entries = spread * jax.random.normal(rng, dims, jnp.float32)
    if cuts:
        entries = entries * shard_levels(rng, dims, cuts, -0.22, 0.18)
    return jnp.clip(entries, -reach, reach).astype(kind)


def setup_inputs(seed: int = 0) -> dict:
    seeds = jax.random.split(jax.random.key(seed), 6)
    weights = scatter_about(seeds[0], (SECTIONS, D, D), D ** -0.5, 0.0625, ((0, 2), (1, 4), (2, 4)))
    inputs = draw_inputs(jax.random.fold_in(seeds[5], 71), 0)
    cotangent = scatter_about(seeds[2], (MICRO, EXAMPLES, L, D), 1.0, 6.0, ((1, 4), (3, 4)))
    clip_norm = draw_clip_norm(jax.random.fold_in(seeds[5], 71), 0)
    noise = scatter_about(seeds[4], (SECTIONS, D, D), 1.0, 6.0, ((0, 2), (1, 4), (2, 4)))
    return dict(weights=weights, inputs=inputs, cotangent=cotangent, clip_norm=clip_norm, noise=noise)


def section_backward(incoming_gradient, weight_matrix):
    flat = incoming_gradient.reshape(-1, D)
    width_block = D // N_DP
    summed = jnp.zeros(flat.shape, jnp.float32)
    for block_index in range(N_DP):
        low = block_index * width_block
        partial_term = jnp.dot(flat[:, low:low + width_block], weight_matrix[:, low:low + width_block].T, preferred_element_type=jnp.float32)
        rounded = lax.optimization_barrier(partial_term.astype(jnp.bfloat16))
        summed = summed + rounded.astype(jnp.float32)
    renewed = flat.astype(jnp.float32) + summed
    return renewed.astype(jnp.bfloat16).reshape(incoming_gradient.shape)

def token_grams(values):
    wide = values.astype(jnp.float32)
    return jnp.einsum('...ld,...kd->...lk', wide, wide)

def reference(weights, inputs, cotangent, clip_norm, noise):
    incoming_gradient = cotangent
    output_grads = [None] * SECTIONS
    for section_index in range(SECTIONS - 1, -1, -1):
        output_grads[section_index] = incoming_gradient
        if section_index > 0:
            incoming_gradient = section_backward(incoming_gradient, weights[section_index])
    norm_square = jnp.zeros((MICRO, EXAMPLES), jnp.float32)
    for section_index in range(SECTIONS):
        input_gram = token_grams(inputs[section_index])
        grad_gram = token_grams(output_grads[section_index])
        norm_square = norm_square + lax.optimization_barrier(jnp.sum(input_gram * grad_gram, axis=(2, 3)))
    bound = clip_norm[0]
    scale_terms = bound / jnp.maximum(jnp.sqrt(norm_square), bound)
    noise_weight = 1.5 / D
    results = []
    for section_index in range(SECTIONS):
        clipped = (inputs[section_index].astype(jnp.float32) * scale_terms[:, :, None, None]).astype(jnp.bfloat16)
        summed = jnp.dot(clipped.reshape(-1, D).T, output_grads[section_index].reshape(-1, D), preferred_element_type=jnp.float32)
        results.append((summed + noise_weight * bound * noise[section_index].astype(jnp.float32)) / (MICRO * EXAMPLES))
    return (jnp.stack(results), scale_terms)
```

```python
import jax
import jax.numpy as jnp
from jax import lax
from jax.experimental import pallas as pl
from jax.experimental.pallas import tpu as pltpu
from jax.sharding import PartitionSpec as P


def shifted(value, axis, steps):
    count = lax.axis_size(axis)
    first, last = (max(0, -steps), min(count, count - steps))
    return lax.ppermute(value, axis, [(source, source + steps) for source in range(first, last)])


def local(weights, inputs, cotangent, clip_norm, noise):
    section_count = lax.axis_size("pipe")
    section_index = lax.axis_index("pipe")
    group_count = lax.axis_size("dp")
    weight_block = weights[0]
    local_inputs = inputs[0]
    micro_count, example_count, length_count, width_part = local_inputs.shape
    token_count = example_count * length_count
    column_part = weight_block.shape[1]
    full_width = column_part * group_count
    partial_grams = jnp.einsum(
        "mbld,mbkd->mblk", local_inputs, local_inputs, preferred_element_type=jnp.float32
    )
    input_grams = lax.psum(partial_grams.astype(jnp.bfloat16), "tensor").astype(jnp.float32)
    received = jnp.zeros((example_count, length_count, width_part), jnp.bfloat16)
    norm_part = jnp.zeros((micro_count, example_count), jnp.float32)
    stored = jnp.zeros((micro_count, group_count * token_count, column_part), jnp.bfloat16)
    micro_ids = jnp.arange(micro_count)
    for step_number in range(micro_count + section_count - 1):
        position = step_number - (section_count - 1 - section_index)
        is_running = jnp.logical_and(position >= 0, position < micro_count)
        chosen = jnp.clip(position, 0, micro_count - 1)
        incoming = lax.dynamic_index_in_dim(cotangent, chosen, 0, keepdims=False)
        current = jnp.where(section_index == section_count - 1, incoming, received)
        incoming_gradient = lax.all_gather(current, "tensor", axis=2, tiled=True)
        grad_grams = jnp.einsum(
            "xeh,xph->xep", incoming_gradient, incoming_gradient, preferred_element_type=jnp.float32
        )
        own_grams = lax.dynamic_index_in_dim(input_grams, chosen, 0, keepdims=False)
        section_terms = jnp.sum(grad_grams * own_grams, axis=(1, 2))
        picked = jnp.logical_and(is_running, micro_ids == chosen)
        norm_part = norm_part + jnp.where(picked[:, None], section_terms[None, :], 0.0)
        by_block = incoming_gradient.reshape(token_count, group_count, column_part)
        scattered_rows = lax.all_to_all(
            by_block, "dp", split_axis=1, concat_axis=0, tiled=True
        ).reshape(group_count * token_count, column_part)
        stored = jnp.where(
            is_running, lax.dynamic_update_index_in_dim(stored, scattered_rows, chosen, 0), stored
        )
        if step_number < micro_count + section_count - 2:
            summed = lax.psum_scatter(
                lax.dot_general(
                    scattered_rows,
                    weight_block,
                    (((1,), (1,)), ((), ())),
                    preferred_element_type=jnp.float32,
                ).astype(jnp.bfloat16),
                "dp",
                scatter_dimension=0,
                tiled=True,
            ).astype(jnp.float32)
            updated = current.reshape(token_count, width_part).astype(jnp.float32) + summed
            outgoing = updated.astype(jnp.bfloat16).reshape(example_count, length_count, width_part)
            received = shifted(outgoing, "pipe", -1)
    bound = clip_norm[0]
    totals = lax.psum(norm_part, "pipe")
    scale_terms = bound / jnp.maximum(jnp.sqrt(totals), bound)
    own_clipped = (local_inputs.astype(jnp.float32) * scale_terms[:, :, None, None]).astype(
        jnp.bfloat16
    )
    clipped = lax.all_gather(own_clipped, "dp", axis=1, tiled=True)
    flat_inputs = clipped.reshape(micro_count * group_count * token_count, width_part)
    flat_grads = stored.reshape(micro_count * group_count * token_count, column_part)
    summed_grad = lax.dot_general(
        flat_inputs, flat_grads, (((0,), (0,)), ((), ())), preferred_element_type=jnp.float32
    )
    noise_weight = 1.5 / full_width
    per_example_sum = micro_count * group_count * example_count
    final_output = (
        summed_grad + noise_weight * bound * noise[0].astype(jnp.float32)
    ) / per_example_sum
    return (final_output[None], scale_terms)


MESH = pl.DeviceIdType.MESH
CHUNKS = 4


def exchange_kernel(
    bound_ref, w_hbm, x_ref, cot_ref,
    xs_ref, factor_ref, g_ref,
    w_ref, xg, zb1, zb2, g1c, bt, rs, gin_send, gin, nz, fb,
    w_sem, w_recv, x_sem, x_recv, loc_sem, zs, zr, as1, ar1, as2, ar2,
    rs_send, rs_recv, gs, gr, ns, nr, fs, fr, pair_send, pair_recv,
):
    p, d, t = lax.axis_index("pipe"), lax.axis_index("dp"), lax.axis_index("tensor")
    sibling = 1 - p
    xn = d + 1 - 2 * lax.rem(d, 2)
    yn = lax.rem(d + 2, 4)
    diagonal = 3 - d
    chunk_rows, width = cot_ref.shape[2], cot_ref.shape[3]
    tokens = CHUNKS * chunk_rows
    half = tokens // 2

    def remote(source, target, send, recv, place):
        return pltpu.make_async_remote_copy(
            src_ref=source, dst_ref=target, send_sem=send, recv_sem=recv,
            device_id=place, device_id_type=MESH,
        )

    barrier = pltpu.get_barrier_semaphore()
    places = [(sibling, d, t)]
    for core in (p, sibling):
        for step in range(1, 4):
            places.append((core, d, lax.rem(t + step, 4)))
            places.append((core, lax.rem(d + step, 4), t))
    for place in places:
        pl.semaphore_signal(barrier, inc=1, device_id=place, device_id_type=MESH)
    pl.semaphore_wait(barrier, len(places))

    def z_send(buf, phase, c, s, way):
        place = (p, d, lax.rem(t + (1 if way == 0 else 3), 4))
        return remote(buf.at[s, c], buf.at[s, c], zs.at[phase, c, s, way], zr.at[phase, c, s], place)

    def own_send(buf, phase, c):
        @pl.when(t < 3)
        def _():
            z_send(buf, phase, c, t, 0).start()

        @pl.when(t > 0)
        def _():
            z_send(buf, phase, c, t, 1).start()

    def spread_remote(phase, c, k):
        if phase == 0:
            return remote(zb1.at[k, c], g1c.at[d, c], as1.at[c, k], ar1.at[c, d], (p, k, t))
        return remote(zb2.at[k, c], g_ref.at[p, d, c], as2.at[c, k], ar2.at[p, d, c], (0, k, t))

    def spread_local(phase, c, k):
        if phase == 0:
            return pltpu.make_async_copy(zb1.at[k, c], g1c.at[d, c], ar1.at[c, d])
        return pltpu.make_async_copy(zb2.at[k, c], g_ref.at[p, d, c], ar2.at[p, d, c])

    def stays(phase, k):
        return k == d if phase == 0 else jnp.logical_and(k == d, p == 0)

    def spread(phase, c, k):
        @pl.when(stays(phase, k))
        def _():
            spread_local(phase, c, k).start()

        @pl.when(jnp.logical_not(stays(phase, k)))
        def _():
            spread_remote(phase, c, k).start()

    def arrivals(buf, phase, c, distance):
        low, high = t - distance, t + distance

        @pl.when(low >= 0)
        def _():
            z_send(buf, phase, c, low, 0).wait_recv()

            @pl.when(t < 3)
            def _():
                z_send(buf, phase, c, low, 0).start()

            spread(phase, c, low)

        @pl.when(high <= 3)
        def _():
            z_send(buf, phase, c, high, 1).wait_recv()

            @pl.when(t > 0)
            def _():
                z_send(buf, phase, c, high, 1).start()

            spread(phase, c, high)

    own = [
        pltpu.make_async_copy(cot_ref.at[p], zb1.at[t], loc_sem.at[0]),
        pltpu.make_async_copy(x_ref, xg.at[d], loc_sem.at[1]),
    ]
    for copy in own:
        copy.start()
    own[0].wait()
    own_send(zb1, 0, 0)
    spread(0, 0, t)

    w_local = pltpu.make_async_copy(w_hbm, w_ref, loc_sem.at[2])
    w_remote = remote(w_hbm, w_ref, w_sem.at[0], w_recv.at[0], (sibling, d, t))

    @pl.when(p == 1)
    def _():
        w_remote.start()
        w_local.start()

    x_sends = [
        remote(x_ref, xg.at[d], x_sem.at[0], x_recv.at[0], (p, xn, t)),
        remote(x_ref, xg.at[d], x_sem.at[1], x_recv.at[1], (p, yn, t)),
    ]
    for copy in x_sends:
        copy.start()

    def gram(block):
        return lax.dot_general(
            block, block, (((1,), (1,)), ((), ())), preferred_element_type=jnp.float32
        )

    for m in range(2):
        gin_send[m] = gram(x_ref[m]).astype(jnp.bfloat16)
    gram_sends = []
    for core in range(2):
        for step in range(4):
            place = (lax.rem(p + core, 2), d, lax.rem(t + step, 4))
            if core or step:
                index = core * 4 + step
                gram_sends.append(
                    remote(gin_send.at[place[0]], gin.at[p, t], gs.at[index], gr.at[index], place)
                )
    for copy in gram_sends:
        copy.start()
    gin[p, t] = gin_send[p]

    def first_round(c, carry):
        arrivals(zb1, 0, c, 1)
        arrivals(zb1, 0, c, 2)

        @pl.when(c < CHUNKS - 1)
        def _():
            own_send(zb1, 0, c + 1)
            spread(0, c + 1, t)

        arrivals(zb1, 0, c, 3)

        @pl.when(c == 0)
        def _():
            @pl.when(p == 1)
            def _():
                w_local.wait()

            @pl.when(p == 0)
            def _():
                w_remote.wait_recv()

        for j in range(4):
            @pl.when(d == j)
            def _():
                spread_local(0, c, d).wait()

            @pl.when(d != j)
            def _():
                remote(
                    zb1.at[0, c], g1c.at[j, c], as1.at[c, 0], ar1.at[c, j], (p, lax.rem(d + 1, 4), t)
                ).wait_recv()
        rows = jnp.concatenate([g1c[j, c] for j in range(4)], axis=0)

        def columns(n, inner):
            start = pl.multiple_of(n * 256, 256)
            terms = lax.dot_general(
                rows, w_ref[pl.ds(start, 256), :], (((1,), (1,)), ((), ())),
                preferred_element_type=jnp.float32,
            ).astype(jnp.bfloat16)
            for j in range(4):
                bt[j, c, :, pl.ds(start, 256)] = terms[j * chunk_rows:(j + 1) * chunk_rows]
            return inner

        lax.fori_loop(0, width // 256, columns, 0)
        for step in (3, 1, 2):
            reduce_send(c, step).start()
        return carry

    def reduce_send(c, step):
        target = lax.rem(d + step, 4)
        return remote(
            bt.at[target, c], rs.at[step - 1, c],
            rs_send.at[c, step - 1], rs_recv.at[c, step - 1], (p, target, t),
        )

    lax.fori_loop(0, CHUNKS, first_round, 0)

    pair_remote = remote(g1c, g_ref.at[0], pair_send.at[0], pair_recv.at[0], (sibling, d, t))
    pair_local = pltpu.make_async_copy(g1c, g_ref.at[1], loc_sem.at[3])

    @pl.when(p == 0)
    def _():
        pair_remote.start()

    @pl.when(p == 1)
    def _():
        pair_local.start()

    def make_own(c):
        for step in range(1, 4):
            reduce_send(c, step).wait_recv()
        total = zb1[t, c].astype(jnp.float32)
        part = bt[d, c].astype(jnp.float32)
        for step in range(3):
            part = part + rs[step, c].astype(jnp.float32)
        zb2[t, c] = (total + part).astype(jnp.bfloat16)
        own_send(zb2, 1, c)
        spread(1, c, t)

    remote(x_ref, xg.at[xn], x_sem.at[0], x_recv.at[0], (p, xn, t)).wait_recv()
    remote(x_ref, xg.at[yn], x_sem.at[1], x_recv.at[1], (p, yn, t)).wait_recv()
    forwards = [
        remote(xg.at[xn, 0], xg.at[xn, 0], x_sem.at[2], x_recv.at[2], (p, yn, t)),
        remote(xg.at[yn, 1], xg.at[yn, 1], x_sem.at[3], x_recv.at[3], (p, xn, t)),
    ]
    for copy in forwards:
        copy.start()

    make_own(0)

    def second_round(c, carry):
        arrivals(zb2, 1, c, 1)
        make_own(c + 1)
        arrivals(zb2, 1, c, 2)
        arrivals(zb2, 1, c, 3)
        return carry

    lax.fori_loop(0, CHUNKS - 1, second_round, 0)

    for copy in gram_sends:
        copy.wait_recv()
    sums = []
    for section in range(2):
        full = gin[section, 0].astype(jnp.float32)
        for part in range(1, 4):
            full = full + gin[section, part].astype(jnp.float32)
        source = zb2 if section == 0 else zb1
        sums.append(full * gram(jnp.concatenate([source[t, c] for c in range(CHUNKS)], axis=0)))
    products = sums[0] + sums[1]
    row = lax.broadcasted_iota(jnp.int32, (8, 128), 0)
    nz[t] = jnp.where(
        row == 0, jnp.sum(products[:half, :half]), jnp.sum(products[half:, half:])
    )
    norm_sends = [
        remote(nz.at[t], nz.at[t], ns.at[step - 1], nr.at[step - 1], (p, d, lax.rem(t + step, 4)))
        for step in range(1, 4)
    ]
    for copy in norm_sends:
        copy.start()
    arrivals(zb2, 1, CHUNKS - 1, 1)
    for copy in norm_sends:
        copy.wait_recv()
    bound = bound_ref[0]
    square = nz[0] + nz[1] + nz[2] + nz[3]
    fb[p, d] = bound / jnp.maximum(jnp.sqrt(square), bound)
    factor_sends = []
    for core in range(2):
        for step in range(4):
            if core or step:
                index = core * 4 + step
                place = (lax.rem(p + core, 2), lax.rem(d + step, 4), t)
                factor_sends.append(remote(fb.at[p, d], fb.at[p, d], fs.at[index], fr.at[index], place))
    for copy in factor_sends:
        copy.start()
    arrivals(zb2, 1, CHUNKS - 1, 2)
    arrivals(zb2, 1, CHUNKS - 1, 3)
    for copy in factor_sends:
        copy.wait_recv()
    own[1].wait()
    remote(xg.at[xn, 0], xg.at[diagonal, 0], x_sem.at[2], x_recv.at[2], (p, yn, t)).wait_recv()
    remote(xg.at[yn, 1], xg.at[diagonal, 1], x_sem.at[3], x_recv.at[3], (p, xn, t)).wait_recv()

    def scale(index, carry):
        j, m = index // 2, lax.rem(index, 2)
        tile = fb[m, j]
        for e in range(2):
            for piece in range(4):
                spot = (pl.ds(e * half + piece * 16, 16), slice(None))
                block = xg[(j, m) + spot].astype(jnp.float32)
                xs_ref[(m, j) + spot] = (block * tile[e:e + 1, 0:1]).astype(jnp.bfloat16)
        return carry

    lax.fori_loop(0, 8, scale, 0)
    for m in range(2):
        factor_ref[m] = fb[m, d]

    def finish(c, carry):
        for phase, buf in ((0, zb1), (1, zb2)):
            for s in range(4):
                @pl.when(jnp.logical_and(s <= t, t < 3))
                def _():
                    z_send(buf, phase, c, s, 0).wait_send()

                @pl.when(jnp.logical_and(s >= t, t > 0))
                def _():
                    z_send(buf, phase, c, s, 1).wait_send()

                @pl.when(jnp.logical_not(stays(phase, s)))
                def _():
                    spread_remote(phase, c, s).wait_send()

        for step in range(1, 4):
            reduce_send(c, step).wait_send()

        @pl.when(p == 0)
        def _():
            for m in range(2):
                for j in range(4):
                    here = jnp.logical_and(j == d, m == 0)

                    @pl.when(here)
                    def _():
                        spread_local(1, c, d).wait()

                    @pl.when(jnp.logical_not(here))
                    def _():
                        remote(
                            zb2.at[0, c], g_ref.at[m, j, c], as2.at[c, 0], ar2.at[m, j, c], (1, d, t)
                        ).wait_recv()
        return carry

    lax.fori_loop(0, CHUNKS, finish, 0)
    for copy in x_sends + forwards + gram_sends + norm_sends + factor_sends:
        copy.wait_send()

    @pl.when(p == 0)
    def _():
        pair_remote.wait_send()

    @pl.when(p == 1)
    def _():
        w_remote.wait_send()
        pair_local.wait()
        pair_remote.wait_recv()


def fast_local(weights, inputs, cotangent, clip_norm, noise):
    weight_block = weights[0]
    width, column_part = weight_block.shape
    micro_count, example_count, length_count, _ = inputs[0].shape
    tokens = example_count * length_count
    rows = tokens // CHUNKS
    bf16, f32 = jnp.bfloat16, jnp.float32
    x = inputs[0].reshape(micro_count, tokens, width)
    cot = cotangent.reshape(micro_count, CHUNKS, rows, width)
    vmem, dma = pltpu.VMEM, pltpu.SemaphoreType.DMA
    shards = (4, CHUNKS, rows, width)
    clipped, factors, gradients = pl.pallas_call(
        exchange_kernel,
        out_shape=(
            jax.ShapeDtypeStruct((2, 4, tokens, width), bf16),
            jax.ShapeDtypeStruct((2, 8, 128), f32),
            jax.ShapeDtypeStruct((2,) + shards, bf16),
        ),
        in_specs=[
            pl.BlockSpec(memory_space=pltpu.SMEM),
            pl.BlockSpec(memory_space=pl.ANY),
            pl.BlockSpec(memory_space=vmem),
            pl.BlockSpec(memory_space=vmem),
        ],
        out_specs=(
            pl.BlockSpec(memory_space=vmem),
            pl.BlockSpec(memory_space=vmem),
            pl.BlockSpec(memory_space=pl.ANY),
        ),
        scratch_shapes=[
            vmem((width, column_part), bf16),
            vmem((4, 2, tokens, width), bf16),
            vmem(shards, bf16), vmem(shards, bf16), vmem(shards, bf16), vmem(shards, bf16),
            vmem((3,) + shards[1:], bf16),
            vmem((2, tokens, tokens), bf16),
            vmem((2, 4, tokens, tokens), bf16),
            vmem((4, 8, 128), f32),
            vmem((2, 4, 8, 128), f32),
            dma((1,)), dma((1,)), dma((4,)), dma((4,)), dma((4,)),
            dma((2, CHUNKS, 4, 2)), dma((2, CHUNKS, 4)),
            dma((CHUNKS, 4)), dma((CHUNKS, 4)), dma((CHUNKS, 4)), dma((2, 4, CHUNKS)),
            dma((CHUNKS, 3)), dma((CHUNKS, 3)),
            dma((8,)), dma((8,)), dma((3,)), dma((3,)), dma((8,)), dma((8,)),
            dma((1,)), dma((1,)),
        ],
        compiler_params=pltpu.CompilerParams(
            collective_id=0, has_side_effects=True, vmem_limit_bytes=50 * 1024 * 1024
        ),
        name="exchange",
    )(clip_norm, weight_block, x, cot)
    total = lax.dot_general(
        clipped.reshape(-1, width), gradients.reshape(-1, column_part),
        (((0,), (0,)), ((), ())), preferred_element_type=f32,
    )
    bound = clip_norm[0]
    noise_weight = 1.5 / (column_part * 4)
    final_output = (total + noise_weight * bound * noise[0].astype(f32)) / (2 * 4 * example_count)
    return (final_output[None], factors[:, :example_count, 0])


def solution(mesh):
    in_specs = (
        P("pipe", "tensor", "dp"),
        P("pipe", None, "dp", None, "tensor"),
        P(None, "dp", None, "tensor"),
        P(),
        P("pipe", "tensor", "dp"),
    )
    out_specs = (P("pipe", "tensor", "dp"), P(None, "dp"))
    fits = mesh.shape["pipe"] == 2 and mesh.shape["dp"] == 4 and mesh.shape["tensor"] == 4
    program = fast_local if fits else local
    return jax.shard_map(
        program, mesh=mesh, in_specs=in_specs, out_specs=out_specs, check_vma=False)
```

```python
import jax
import jax.numpy as jnp
from jax import lax
from jax.experimental import pallas as pl
from jax.experimental.pallas import tpu as pltpu
from jax.sharding import PartitionSpec as P


def shifted(value, axis, steps):
    count = lax.axis_size(axis)
    first, last = (max(0, -steps), min(count, count - steps))
    return lax.ppermute(value, axis, [(source, source + steps) for source in range(first, last)])


def local(weights, inputs, cotangent, clip_norm, noise):
    section_count = lax.axis_size("pipe")
    section_index = lax.axis_index("pipe")
    group_count = lax.axis_size("dp")
    weight_block = weights[0]
    local_inputs = inputs[0]
    micro_count, example_count, length_count, width_part = local_inputs.shape
    token_count = example_count * length_count
    column_part = weight_block.shape[1]
    full_width = column_part * group_count
    partial_grams = jnp.einsum(
        "mbld,mbkd->mblk", local_inputs, local_inputs, preferred_element_type=jnp.float32
    )
    input_grams = lax.psum(partial_grams.astype(jnp.bfloat16), "tensor").astype(jnp.float32)
    received = jnp.zeros((example_count, length_count, width_part), jnp.bfloat16)
    norm_part = jnp.zeros((micro_count, example_count), jnp.float32)
    stored = jnp.zeros((micro_count, group_count * token_count, column_part), jnp.bfloat16)
    micro_ids = jnp.arange(micro_count)
    for step_number in range(micro_count + section_count - 1):
        position = step_number - (section_count - 1 - section_index)
        is_running = jnp.logical_and(position >= 0, position < micro_count)
        chosen = jnp.clip(position, 0, micro_count - 1)
        incoming = lax.dynamic_index_in_dim(cotangent, chosen, 0, keepdims=False)
        current = jnp.where(section_index == section_count - 1, incoming, received)
        incoming_gradient = lax.all_gather(current, "tensor", axis=2, tiled=True)
        grad_grams = jnp.einsum(
            "xeh,xph->xep", incoming_gradient, incoming_gradient, preferred_element_type=jnp.float32
        )
        own_grams = lax.dynamic_index_in_dim(input_grams, chosen, 0, keepdims=False)
        section_terms = jnp.sum(grad_grams * own_grams, axis=(1, 2))
        picked = jnp.logical_and(is_running, micro_ids == chosen)
        norm_part = norm_part + jnp.where(picked[:, None], section_terms[None, :], 0.0)
        by_block = incoming_gradient.reshape(token_count, group_count, column_part)
        scattered_rows = lax.all_to_all(
            by_block, "dp", split_axis=1, concat_axis=0, tiled=True
        ).reshape(group_count * token_count, column_part)
        stored = jnp.where(
            is_running, lax.dynamic_update_index_in_dim(stored, scattered_rows, chosen, 0), stored
        )
        if step_number < micro_count + section_count - 2:
            summed = lax.psum_scatter(
                lax.dot_general(
                    scattered_rows,
                    weight_block,
                    (((1,), (1,)), ((), ())),
                    preferred_element_type=jnp.float32,
                ).astype(jnp.bfloat16),
                "dp",
                scatter_dimension=0,
                tiled=True,
            ).astype(jnp.float32)
            updated = current.reshape(token_count, width_part).astype(jnp.float32) + summed
            outgoing = updated.astype(jnp.bfloat16).reshape(example_count, length_count, width_part)
            received = shifted(outgoing, "pipe", -1)
    bound = clip_norm[0]
    totals = lax.psum(norm_part, "pipe")
    scale_terms = bound / jnp.maximum(jnp.sqrt(totals), bound)
    own_clipped = (local_inputs.astype(jnp.float32) * scale_terms[:, :, None, None]).astype(
        jnp.bfloat16
    )
    clipped = lax.all_gather(own_clipped, "dp", axis=1, tiled=True)
    flat_inputs = clipped.reshape(micro_count * group_count * token_count, width_part)
    flat_grads = stored.reshape(micro_count * group_count * token_count, column_part)
    summed_grad = lax.dot_general(
        flat_inputs, flat_grads, (((0,), (0,)), ((), ())), preferred_element_type=jnp.float32
    )
    noise_weight = 1.5 / full_width
    per_example_sum = micro_count * group_count * example_count
    final_output = (
        summed_grad + noise_weight * bound * noise[0].astype(jnp.float32)
    ) / per_example_sum
    return (final_output[None], scale_terms)


MESH = pl.DeviceIdType.MESH
CHUNKS = 4


def exchange_kernel(
    bound_ref, w_hbm, x_ref, cot_ref,
    xs_ref, factor_ref, g_ref,
    w_ref, xg, zb1, zb2, g1c, bt, rs, gin_send, gin, nz, fb,
    w_sem, w_recv, x_sem, x_recv, loc_sem, zs, zr, as1, ar1, as2, ar2,
    rs_send, rs_recv, gs, gr, ns, nr, fs, fr, pair_send, pair_recv,
):
    p, d, t = lax.axis_index("pipe"), lax.axis_index("dp"), lax.axis_index("tensor")
    sibling = 1 - p
    xn = d + 1 - 2 * lax.rem(d, 2)
    yn = lax.rem(d + 2, 4)
    diagonal = 3 - d
    chunk_rows, width = cot_ref.shape[2], cot_ref.shape[3]
    tokens = CHUNKS * chunk_rows
    half = tokens // 2

    def remote(source, target, send, recv, place):
        return pltpu.make_async_remote_copy(
            src_ref=source, dst_ref=target, send_sem=send, recv_sem=recv,
            device_id=place, device_id_type=MESH,
        )

    barrier = pltpu.get_barrier_semaphore()
    places = [(sibling, d, t)]
    for core in (p, sibling):
        for step in range(1, 4):
            places.append((core, d, lax.rem(t + step, 4)))
            places.append((core, lax.rem(d + step, 4), t))
    for place in places:
        pl.semaphore_signal(barrier, inc=1, device_id=place, device_id_type=MESH)
    pl.semaphore_wait(barrier, len(places))

    def z_send(buf, phase, c, s, way):
        place = (p, d, lax.rem(t + (1 if way == 0 else 3), 4))
        return remote(buf.at[s, c], buf.at[s, c], zs.at[phase, c, s, way], zr.at[phase, c, s], place)

    def own_send(buf, phase, c):
        @pl.when(t < 3)
        def _():
            z_send(buf, phase, c, t, 0).start()

        @pl.when(t > 0)
        def _():
            z_send(buf, phase, c, t, 1).start()

    def spread_remote(phase, c, k):
        if phase == 0:
            return remote(zb1.at[k, c], g1c.at[d, c], as1.at[c, k], ar1.at[c, d], (p, k, t))
        return remote(zb2.at[k, c], g_ref.at[p, d, c], as2.at[c, k], ar2.at[p, d, c], (0, k, t))

    def spread_local(phase, c, k):
        if phase == 0:
            return pltpu.make_async_copy(zb1.at[k, c], g1c.at[d, c], ar1.at[c, d])
        return pltpu.make_async_copy(zb2.at[k, c], g_ref.at[p, d, c], ar2.at[p, d, c])

    def stays(phase, k):
        return k == d if phase == 0 else jnp.logical_and(k == d, p == 0)

    def spread(phase, c, k):
        @pl.when(stays(phase, k))
        def _():
            spread_local(phase, c, k).start()

        @pl.when(jnp.logical_not(stays(phase, k)))
        def _():
            spread_remote(phase, c, k).start()

    def arrivals(buf, phase, c, distance):
        low, high = t - distance, t + distance

        @pl.when(low >= 0)
        def _():
            z_send(buf, phase, c, low, 0).wait_recv()

            @pl.when(t < 3)
            def _():
                z_send(buf, phase, c, low, 0).start()

            spread(phase, c, low)

        @pl.when(high <= 3)
        def _():
            z_send(buf, phase, c, high, 1).wait_recv()

            @pl.when(t > 0)
            def _():
                z_send(buf, phase, c, high, 1).start()

            spread(phase, c, high)

    own = [
        pltpu.make_async_copy(cot_ref.at[p], zb1.at[t], loc_sem.at[0]),
        pltpu.make_async_copy(x_ref, xg.at[d], loc_sem.at[1]),
    ]
    for copy in own:
        copy.start()
    own[0].wait()
    own_send(zb1, 0, 0)
    spread(0, 0, t)

    w_local = pltpu.make_async_copy(w_hbm, w_ref, loc_sem.at[2])
    w_remote = remote(w_hbm, w_ref, w_sem.at[0], w_recv.at[0], (sibling, d, t))

    @pl.when(p == 1)
    def _():
        w_remote.start()
        w_local.start()

    x_sends = [
        remote(x_ref.at[m], xg.at[d, m], x_sem.at[2 * m + i], x_recv.at[2 * m + i], (p, near, t))
        for m in range(2) for i, near in enumerate((xn, yn))
    ]
    for copy in x_sends[:2]:
        copy.start()

    def gram(block):
        return lax.dot_general(
            block, block, (((1,), (1,)), ((), ())), preferred_element_type=jnp.float32
        )

    for m in range(2):
        gin_send[m] = gram(x_ref[m]).astype(jnp.bfloat16)
    gram_sends = []
    for core in range(2):
        for step in range(4):
            place = (lax.rem(p + core, 2), d, lax.rem(t + step, 4))
            if core or step:
                index = core * 4 + step
                gram_sends.append(
                    remote(gin_send.at[place[0]], gin.at[p, t], gs.at[index], gr.at[index], place)
                )
    for copy in gram_sends:
        copy.start()
    gin[p, t] = gin_send[p]

    def first_round(c, carry):
        @pl.when(c < CHUNKS)
        def _():
            arrivals(zb1, 0, c, 1)
            arrivals(zb1, 0, c, 2)

            @pl.when(c < CHUNKS - 1)
            def _():
                own_send(zb1, 0, c + 1)
                spread(0, c + 1, t)

            arrivals(zb1, 0, c, 3)

        @pl.when(c > 0)
        def _():
            block_terms(c - 1)

        return carry

    def block_terms(c):
        @pl.when(c == 0)
        def _():
            @pl.when(p == 1)
            def _():
                w_local.wait()

            @pl.when(p == 0)
            def _():
                w_remote.wait_recv()

        for j in range(4):
            @pl.when(d == j)
            def _():
                spread_local(0, c, d).wait()

            @pl.when(d != j)
            def _():
                remote(
                    zb1.at[0, c], g1c.at[j, c], as1.at[c, 0], ar1.at[c, j], (p, lax.rem(d + 1, 4), t)
                ).wait_recv()
        rows = jnp.concatenate([g1c[j, c] for j in range(4)], axis=0)

        def columns(n, inner):
            start = pl.multiple_of(n * 256, 256)
            terms = lax.dot_general(
                rows, w_ref[pl.ds(start, 256), :], (((1,), (1,)), ((), ())),
                preferred_element_type=jnp.float32,
            ).astype(jnp.bfloat16)
            for j in range(4):
                bt[j, c, :, pl.ds(start, 256)] = terms[j * chunk_rows:(j + 1) * chunk_rows]
            return inner

        lax.fori_loop(0, width // 256, columns, 0)
        for step in (3, 1, 2):
            reduce_send(c, step).start()

    def reduce_send(c, step):
        target = lax.rem(d + step, 4)
        return remote(
            bt.at[target, c], rs.at[step - 1, c],
            rs_send.at[c, step - 1], rs_recv.at[c, step - 1], (p, target, t),
        )

    lax.fori_loop(0, CHUNKS + 1, first_round, 0)

    pair_remote = remote(g1c, g_ref.at[0], pair_send.at[0], pair_recv.at[0], (sibling, d, t))
    pair_local = pltpu.make_async_copy(g1c, g_ref.at[1], loc_sem.at[3])

    @pl.when(p == 0)
    def _():
        pair_remote.start()

    @pl.when(p == 1)
    def _():
        pair_local.start()

    def make_own(c):
        for step in range(1, 4):
            reduce_send(c, step).wait_recv()
        total = zb1[t, c].astype(jnp.float32)
        part = bt[d, c].astype(jnp.float32)
        for step in range(3):
            part = part + rs[step, c].astype(jnp.float32)
        zb2[t, c] = (total + part).astype(jnp.bfloat16)
        own_send(zb2, 1, c)
        spread(1, c, t)

    def x_wait(m, i, slot, place):
        index = 2 * m + i
        remote(x_ref.at[m], xg.at[slot, m], x_sem.at[index], x_recv.at[index], (p, place, t)).wait_recv()

    x_wait(0, 0, xn, xn)
    x_wait(0, 1, yn, yn)
    forwards = [
        remote(xg.at[xn, 0], xg.at[xn, 0], x_sem.at[4], x_recv.at[4], (p, yn, t)),
        remote(xg.at[yn, 1], xg.at[yn, 1], x_sem.at[5], x_recv.at[5], (p, xn, t)),
    ]
    for copy in x_sends[2:]:
        copy.start()
    forwards[0].start()

    make_own(0)

    def second_round(c, carry):
        arrivals(zb2, 1, c, 1)
        make_own(c + 1)
        arrivals(zb2, 1, c, 2)
        arrivals(zb2, 1, c, 3)
        return carry

    lax.fori_loop(0, CHUNKS - 2, second_round, 0)
    arrivals(zb2, 1, CHUNKS - 2, 1)
    make_own(CHUNKS - 1)
    x_wait(1, 1, yn, yn)
    forwards[1].start()

    for copy in gram_sends:
        copy.wait_recv()
    sums = []
    for section in range(2):
        full = gin[section, 0].astype(jnp.float32)
        for part in range(1, 4):
            full = full + gin[section, part].astype(jnp.float32)
        source = zb2 if section == 0 else zb1
        sums.append(full * gram(jnp.concatenate([source[t, c] for c in range(CHUNKS)], axis=0)))
    products = sums[0] + sums[1]
    row = lax.broadcasted_iota(jnp.int32, (8, 128), 0)
    nz[t] = jnp.where(
        row == 0, jnp.sum(products[:half, :half]), jnp.sum(products[half:, half:])
    )
    norm_sends = [
        remote(nz.at[t], nz.at[t], ns.at[step - 1], nr.at[step - 1], (p, d, lax.rem(t + step, 4)))
        for step in range(1, 4)
    ]
    for copy in norm_sends:
        copy.start()
    arrivals(zb2, 1, CHUNKS - 2, 2)
    arrivals(zb2, 1, CHUNKS - 2, 3)
    for copy in norm_sends:
        copy.wait_recv()
    bound = bound_ref[0]
    square = nz[0] + nz[1] + nz[2] + nz[3]
    fb[p, d] = bound / jnp.maximum(jnp.sqrt(square), bound)
    factor_sends = []
    for core in range(2):
        for step in range(4):
            if core or step:
                index = core * 4 + step
                place = (lax.rem(p + core, 2), lax.rem(d + step, 4), t)
                factor_sends.append(remote(fb.at[p, d], fb.at[p, d], fs.at[index], fr.at[index], place))
    for copy in factor_sends:
        copy.start()
    for distance in range(1, 4):
        arrivals(zb2, 1, CHUNKS - 1, distance)
    for copy in factor_sends:
        copy.wait_recv()
    own[1].wait()
    x_wait(1, 0, xn, xn)
    remote(xg.at[xn, 0], xg.at[diagonal, 0], x_sem.at[4], x_recv.at[4], (p, yn, t)).wait_recv()
    remote(xg.at[yn, 1], xg.at[diagonal, 1], x_sem.at[5], x_recv.at[5], (p, xn, t)).wait_recv()

    def scale(index, carry):
        j, m = index // 2, lax.rem(index, 2)
        tile = fb[m, j]
        for e in range(2):
            for piece in range(4):
                spot = (pl.ds(e * half + piece * 16, 16), slice(None))
                block = xg[(j, m) + spot].astype(jnp.float32)
                xs_ref[(m, j) + spot] = (block * tile[e:e + 1, 0:1]).astype(jnp.bfloat16)
        return carry

    lax.fori_loop(0, 8, scale, 0)
    for m in range(2):
        factor_ref[m] = fb[m, d]

    def finish(c, carry):
        for phase, buf in ((0, zb1), (1, zb2)):
            for s in range(4):
                @pl.when(jnp.logical_and(s <= t, t < 3))
                def _():
                    z_send(buf, phase, c, s, 0).wait_send()

                @pl.when(jnp.logical_and(s >= t, t > 0))
                def _():
                    z_send(buf, phase, c, s, 1).wait_send()

                @pl.when(jnp.logical_not(stays(phase, s)))
                def _():
                    spread_remote(phase, c, s).wait_send()

        for step in range(1, 4):
            reduce_send(c, step).wait_send()

        @pl.when(p == 0)
        def _():
            for m in range(2):
                for j in range(4):
                    here = jnp.logical_and(j == d, m == 0)

                    @pl.when(here)
                    def _():
                        spread_local(1, c, d).wait()

                    @pl.when(jnp.logical_not(here))
                    def _():
                        remote(
                            zb2.at[0, c], g_ref.at[m, j, c], as2.at[c, 0], ar2.at[m, j, c], (1, d, t)
                        ).wait_recv()
        return carry

    lax.fori_loop(0, CHUNKS, finish, 0)
    for copy in x_sends + forwards + gram_sends + norm_sends + factor_sends:
        copy.wait_send()

    @pl.when(p == 0)
    def _():
        pair_remote.wait_send()

    @pl.when(p == 1)
    def _():
        w_remote.wait_send()
        pair_local.wait()
        pair_remote.wait_recv()


def fast_local(weights, inputs, cotangent, clip_norm, noise):
    weight_block = weights[0]
    width, column_part = weight_block.shape
    micro_count, example_count, length_count, _ = inputs[0].shape
    tokens = example_count * length_count
    rows = tokens // CHUNKS
    bf16, f32 = jnp.bfloat16, jnp.float32
    x = inputs[0].reshape(micro_count, tokens, width)
    cot = cotangent.reshape(micro_count, CHUNKS, rows, width)
    vmem, dma = pltpu.VMEM, pltpu.SemaphoreType.DMA
    shards = (4, CHUNKS, rows, width)
    clipped, factors, gradients = pl.pallas_call(
        exchange_kernel,
        out_shape=(
            jax.ShapeDtypeStruct((2, 4, tokens, width), bf16),
            jax.ShapeDtypeStruct((2, 8, 128), f32),
            jax.ShapeDtypeStruct((2,) + shards, bf16),
        ),
        in_specs=[
            pl.BlockSpec(memory_space=pltpu.SMEM),
            pl.BlockSpec(memory_space=pl.ANY),
            pl.BlockSpec(memory_space=vmem),
            pl.BlockSpec(memory_space=vmem),
        ],
        out_specs=(
            pl.BlockSpec(memory_space=vmem),
            pl.BlockSpec(memory_space=vmem),
            pl.BlockSpec(memory_space=pl.ANY),
        ),
        scratch_shapes=[
            vmem((width, column_part), bf16),
            vmem((4, 2, tokens, width), bf16),
            vmem(shards, bf16), vmem(shards, bf16), vmem(shards, bf16), vmem(shards, bf16),
            vmem((3,) + shards[1:], bf16),
            vmem((2, tokens, tokens), bf16),
            vmem((2, 4, tokens, tokens), bf16),
            vmem((4, 8, 128), f32),
            vmem((2, 4, 8, 128), f32),
            dma((1,)), dma((1,)), dma((6,)), dma((6,)), dma((4,)),
            dma((2, CHUNKS, 4, 2)), dma((2, CHUNKS, 4)),
            dma((CHUNKS, 4)), dma((CHUNKS, 4)), dma((CHUNKS, 4)), dma((2, 4, CHUNKS)),
            dma((CHUNKS, 3)), dma((CHUNKS, 3)),
            dma((8,)), dma((8,)), dma((3,)), dma((3,)), dma((8,)), dma((8,)),
            dma((1,)), dma((1,)),
        ],
        compiler_params=pltpu.CompilerParams(
            collective_id=0, has_side_effects=True, vmem_limit_bytes=50 * 1024 * 1024
        ),
        name="exchange",
    )(clip_norm, weight_block, x, cot)
    total = lax.dot_general(
        clipped.reshape(-1, width), gradients.reshape(-1, column_part),
        (((0,), (0,)), ((), ())), preferred_element_type=f32,
    )
    bound = clip_norm[0]
    noise_weight = 1.5 / (column_part * 4)
    final_output = (total + noise_weight * bound * noise[0].astype(f32)) / (2 * 4 * example_count)
    return (final_output[None], factors[:, :example_count, 0])


def solution(mesh):
    in_specs = (
        P("pipe", "tensor", "dp"),
        P("pipe", None, "dp", None, "tensor"),
        P(None, "dp", None, "tensor"),
        P(),
        P("pipe", "tensor", "dp"),
    )
    out_specs = (P("pipe", "tensor", "dp"), P(None, "dp"))
    fits = mesh.shape["pipe"] == 2 and mesh.shape["dp"] == 4 and mesh.shape["tensor"] == 4
    program = fast_local if fits else local
    return jax.shard_map(
        program, mesh=mesh, in_specs=in_specs, out_specs=out_specs, check_vma=False)
```

```python
import jax
import jax.numpy as jnp
from jax import lax
from jax.experimental import pallas as pl
from jax.experimental.pallas import tpu as pltpu
from jax.sharding import PartitionSpec as P


def shifted(value, axis, steps):
    count = lax.axis_size(axis)
    first, last = (max(0, -steps), min(count, count - steps))
    return lax.ppermute(value, axis, [(source, source + steps) for source in range(first, last)])


def local(weights, inputs, cotangent, clip_norm, noise):
    section_count = lax.axis_size("pipe")
    section_index = lax.axis_index("pipe")
    group_count = lax.axis_size("dp")
    weight_block = weights[0]
    local_inputs = inputs[0]
    micro_count, example_count, length_count, width_part = local_inputs.shape
    token_count = example_count * length_count
    column_part = weight_block.shape[1]
    full_width = column_part * group_count
    partial_grams = jnp.einsum(
        "mbld,mbkd->mblk", local_inputs, local_inputs, preferred_element_type=jnp.float32
    )
    input_grams = lax.psum(partial_grams.astype(jnp.bfloat16), "tensor").astype(jnp.float32)
    received = jnp.zeros((example_count, length_count, width_part), jnp.bfloat16)
    norm_part = jnp.zeros((micro_count, example_count), jnp.float32)
    stored = jnp.zeros((micro_count, group_count * token_count, column_part), jnp.bfloat16)
    micro_ids = jnp.arange(micro_count)
    for step_number in range(micro_count + section_count - 1):
        position = step_number - (section_count - 1 - section_index)
        is_running = jnp.logical_and(position >= 0, position < micro_count)
        chosen = jnp.clip(position, 0, micro_count - 1)
        incoming = lax.dynamic_index_in_dim(cotangent, chosen, 0, keepdims=False)
        current = jnp.where(section_index == section_count - 1, incoming, received)
        incoming_gradient = lax.all_gather(current, "tensor", axis=2, tiled=True)
        grad_grams = jnp.einsum(
            "xeh,xph->xep", incoming_gradient, incoming_gradient, preferred_element_type=jnp.float32
        )
        own_grams = lax.dynamic_index_in_dim(input_grams, chosen, 0, keepdims=False)
        section_terms = jnp.sum(grad_grams * own_grams, axis=(1, 2))
        picked = jnp.logical_and(is_running, micro_ids == chosen)
        norm_part = norm_part + jnp.where(picked[:, None], section_terms[None, :], 0.0)
        by_block = incoming_gradient.reshape(token_count, group_count, column_part)
        scattered_rows = lax.all_to_all(
            by_block, "dp", split_axis=1, concat_axis=0, tiled=True
        ).reshape(group_count * token_count, column_part)
        stored = jnp.where(
            is_running, lax.dynamic_update_index_in_dim(stored, scattered_rows, chosen, 0), stored
        )
        if step_number < micro_count + section_count - 2:
            summed = lax.psum_scatter(
                lax.dot_general(
                    scattered_rows,
                    weight_block,
                    (((1,), (1,)), ((), ())),
                    preferred_element_type=jnp.float32,
                ).astype(jnp.bfloat16),
                "dp",
                scatter_dimension=0,
                tiled=True,
            ).astype(jnp.float32)
            updated = current.reshape(token_count, width_part).astype(jnp.float32) + summed
            outgoing = updated.astype(jnp.bfloat16).reshape(example_count, length_count, width_part)
            received = shifted(outgoing, "pipe", -1)
    bound = clip_norm[0]
    totals = lax.psum(norm_part, "pipe")
    scale_terms = bound / jnp.maximum(jnp.sqrt(totals), bound)
    own_clipped = (local_inputs.astype(jnp.float32) * scale_terms[:, :, None, None]).astype(
        jnp.bfloat16
    )
    clipped = lax.all_gather(own_clipped, "dp", axis=1, tiled=True)
    flat_inputs = clipped.reshape(micro_count * group_count * token_count, width_part)
    flat_grads = stored.reshape(micro_count * group_count * token_count, column_part)
    summed_grad = lax.dot_general(
        flat_inputs, flat_grads, (((0,), (0,)), ((), ())), preferred_element_type=jnp.float32
    )
    noise_weight = 1.5 / full_width
    per_example_sum = micro_count * group_count * example_count
    final_output = (
        summed_grad + noise_weight * bound * noise[0].astype(jnp.float32)
    ) / per_example_sum
    return (final_output[None], scale_terms)


MESH = pl.DeviceIdType.MESH
CHUNKS = 4


def exchange_kernel(
    bound_ref, w_hbm, x_ref, cot_ref,
    xs_ref, factor_ref, g_ref,
    w_ref, xg, zb1, zb2, g1c, bt, rs, gin_send, gin, nz, fb,
    w_sem, w_recv, x_sem, x_recv, loc_sem, zs, zr, as1, ar1, as2, ar2,
    rs_send, rs_recv, gs, gr, ns, nr, fs, fr, pair_send, pair_recv,
):
    p, d, t = lax.axis_index("pipe"), lax.axis_index("dp"), lax.axis_index("tensor")
    sibling = 1 - p
    xn = d + 1 - 2 * lax.rem(d, 2)
    yn = lax.rem(d + 2, 4)
    diagonal = 3 - d
    chunk_rows, width = cot_ref.shape[2], cot_ref.shape[3]
    tokens = CHUNKS * chunk_rows
    half = tokens // 2

    def remote(source, target, send, recv, place):
        return pltpu.make_async_remote_copy(
            src_ref=source, dst_ref=target, send_sem=send, recv_sem=recv,
            device_id=place, device_id_type=MESH,
        )

    barrier = pltpu.get_barrier_semaphore()
    places = [(sibling, d, t)]
    for core in (p, sibling):
        for step in range(1, 4):
            places.append((core, d, lax.rem(t + step, 4)))
            places.append((core, lax.rem(d + step, 4), t))
    for place in places:
        pl.semaphore_signal(barrier, inc=1, device_id=place, device_id_type=MESH)
    pl.semaphore_wait(barrier, len(places))

    def z_send(buf, phase, c, s, way):
        place = (p, d, lax.rem(t + (1 if way == 0 else 3), 4))
        return remote(buf.at[s, c], buf.at[s, c], zs.at[phase, c, s, way], zr.at[phase, c, s], place)

    def own_send(buf, phase, c):
        @pl.when(t < 3)
        def _():
            z_send(buf, phase, c, t, 0).start()

        @pl.when(t > 0)
        def _():
            z_send(buf, phase, c, t, 1).start()

    def spread_remote(phase, c, k):
        if phase == 0:
            return remote(zb1.at[k, c], g1c.at[d, c], as1.at[c, k], ar1.at[c, d], (p, k, t))
        return remote(zb2.at[k, c], g_ref.at[p, d, c], as2.at[c, k], ar2.at[p, d, c], (0, k, t))

    def spread_local(phase, c, k):
        if phase == 0:
            return pltpu.make_async_copy(zb1.at[k, c], g1c.at[d, c], ar1.at[c, d])
        return pltpu.make_async_copy(zb2.at[k, c], g_ref.at[p, d, c], ar2.at[p, d, c])

    def stays(phase, k):
        return k == d if phase == 0 else jnp.logical_and(k == d, p == 0)

    def spread(phase, c, k):
        @pl.when(stays(phase, k))
        def _():
            spread_local(phase, c, k).start()

        @pl.when(jnp.logical_not(stays(phase, k)))
        def _():
            spread_remote(phase, c, k).start()

    def arrivals(buf, phase, c, distance):
        low, high = t - distance, t + distance

        @pl.when(low >= 0)
        def _():
            z_send(buf, phase, c, low, 0).wait_recv()

            @pl.when(t < 3)
            def _():
                z_send(buf, phase, c, low, 0).start()

            spread(phase, c, low)

        @pl.when(high <= 3)
        def _():
            z_send(buf, phase, c, high, 1).wait_recv()

            @pl.when(t > 0)
            def _():
                z_send(buf, phase, c, high, 1).start()

            spread(phase, c, high)

    own = [
        pltpu.make_async_copy(cot_ref.at[p], zb1.at[t], loc_sem.at[0]),
        pltpu.make_async_copy(x_ref, xg.at[d], loc_sem.at[1]),
    ]
    for copy in own:
        copy.start()
    own[0].wait()
    own_send(zb1, 0, 0)
    spread(0, 0, t)

    w_local = pltpu.make_async_copy(w_hbm, w_ref, loc_sem.at[2])
    w_remote = remote(w_hbm, w_ref, w_sem.at[0], w_recv.at[0], (sibling, d, t))

    @pl.when(p == 1)
    def _():
        w_remote.start()
        w_local.start()

    x_sends = [
        remote(x_ref.at[m], xg.at[d, m], x_sem.at[2 * m + i], x_recv.at[2 * m + i], (p, near, t))
        for m in range(2) for i, near in enumerate((xn, yn))
    ]
    for copy in x_sends[:2]:
        copy.start()

    def gram(block):
        return lax.dot_general(
            block, block, (((1,), (1,)), ((), ())), preferred_element_type=jnp.float32
        )

    for m in range(2):
        gin_send[m] = gram(x_ref[m]).astype(jnp.bfloat16)
    gram_sends = []
    for core in range(2):
        for step in range(4):
            place = (lax.rem(p + core, 2), d, lax.rem(t + step, 4))
            if core or step:
                index = core * 4 + step
                gram_sends.append(
                    remote(gin_send.at[place[0]], gin.at[p, t], gs.at[index], gr.at[index], place)
                )
    for copy in gram_sends:
        copy.start()
    gin[p, t] = gin_send[p]

    def first_round(c, carry):
        arrivals(zb1, 0, c, 1)
        arrivals(zb1, 0, c, 2)

        @pl.when(c < CHUNKS - 1)
        def _():
            own_send(zb1, 0, c + 1)
            spread(0, c + 1, t)

        arrivals(zb1, 0, c, 3)

        @pl.when(c > 0)
        def _():
            block_terms(c - 1)

        return carry

    def block_terms(c):
        @pl.when(c == 0)
        def _():
            @pl.when(p == 1)
            def _():
                w_local.wait()

            @pl.when(p == 0)
            def _():
                w_remote.wait_recv()

        for j in range(4):
            @pl.when(d == j)
            def _():
                spread_local(0, c, d).wait()

            @pl.when(d != j)
            def _():
                remote(
                    zb1.at[0, c], g1c.at[j, c], as1.at[c, 0], ar1.at[c, j], (p, lax.rem(d + 1, 4), t)
                ).wait_recv()
        rows = jnp.concatenate([g1c[j, c] for j in range(4)], axis=0)

        def columns(n, inner):
            start = pl.multiple_of(n * 256, 256)
            terms = lax.dot_general(
                rows, w_ref[pl.ds(start, 256), :], (((1,), (1,)), ((), ())),
                preferred_element_type=jnp.float32,
            ).astype(jnp.bfloat16)
            for j in range(4):
                bt[j, c, :, pl.ds(start, 256)] = terms[j * chunk_rows:(j + 1) * chunk_rows]
            return inner

        lax.fori_loop(0, width // 256, columns, 0)
        for step in (3, 1, 2):
            reduce_send(c, step).start()

    def reduce_send(c, step):
        target = lax.rem(d + step, 4)
        return remote(
            bt.at[target, c], rs.at[step - 1, c],
            rs_send.at[c, step - 1], rs_recv.at[c, step - 1], (p, target, t),
        )


    def make_own(c):
        for step in range(1, 4):
            reduce_send(c, step).wait_recv()
        total = zb1[t, c].astype(jnp.float32)
        part = bt[d, c].astype(jnp.float32)
        for step in range(3):
            part = part + rs[step, c].astype(jnp.float32)
        zb2[t, c] = (total + part).astype(jnp.bfloat16)
        own_send(zb2, 1, c)
        spread(1, c, t)

    lax.fori_loop(0, CHUNKS, first_round, 0)
    make_own(0)
    block_terms(CHUNKS - 1)

    pair_remote = remote(g1c, g_ref.at[0], pair_send.at[0], pair_recv.at[0], (sibling, d, t))
    pair_local = pltpu.make_async_copy(g1c, g_ref.at[1], loc_sem.at[3])

    @pl.when(p == 0)
    def _():
        pair_remote.start()

    @pl.when(p == 1)
    def _():
        pair_local.start()

    def x_wait(m, i, slot, place):
        index = 2 * m + i
        remote(x_ref.at[m], xg.at[slot, m], x_sem.at[index], x_recv.at[index], (p, place, t)).wait_recv()

    x_wait(0, 0, xn, xn)
    x_wait(0, 1, yn, yn)
    forwards = [
        remote(xg.at[xn, 0], xg.at[xn, 0], x_sem.at[4], x_recv.at[4], (p, yn, t)),
        remote(xg.at[yn, 1], xg.at[yn, 1], x_sem.at[5], x_recv.at[5], (p, xn, t)),
    ]
    for copy in x_sends[2:]:
        copy.start()
    forwards[0].start()


    def second_round(c, carry):
        arrivals(zb2, 1, c, 1)
        make_own(c + 1)
        arrivals(zb2, 1, c, 2)
        arrivals(zb2, 1, c, 3)
        return carry

    lax.fori_loop(0, CHUNKS - 2, second_round, 0)
    arrivals(zb2, 1, CHUNKS - 2, 1)
    make_own(CHUNKS - 1)
    x_wait(1, 1, yn, yn)
    forwards[1].start()

    for copy in gram_sends:
        copy.wait_recv()
    sums = []
    for section in range(2):
        full = gin[section, 0].astype(jnp.float32)
        for part in range(1, 4):
            full = full + gin[section, part].astype(jnp.float32)
        source = zb2 if section == 0 else zb1
        sums.append(full * gram(jnp.concatenate([source[t, c] for c in range(CHUNKS)], axis=0)))
    products = sums[0] + sums[1]
    row = lax.broadcasted_iota(jnp.int32, (8, 128), 0)
    nz[t] = jnp.where(
        row == 0, jnp.sum(products[:half, :half]), jnp.sum(products[half:, half:])
    )
    norm_sends = [
        remote(nz.at[t], nz.at[t], ns.at[step - 1], nr.at[step - 1], (p, d, lax.rem(t + step, 4)))
        for step in range(1, 4)
    ]
    for copy in norm_sends:
        copy.start()
    arrivals(zb2, 1, CHUNKS - 2, 2)
    arrivals(zb2, 1, CHUNKS - 2, 3)
    for copy in norm_sends:
        copy.wait_recv()
    bound = bound_ref[0]
    square = nz[0] + nz[1] + nz[2] + nz[3]
    fb[p, d] = bound / jnp.maximum(jnp.sqrt(square), bound)
    factor_sends = []
    for core in range(2):
        for step in range(4):
            if core or step:
                index = core * 4 + step
                place = (lax.rem(p + core, 2), lax.rem(d + step, 4), t)
                factor_sends.append(remote(fb.at[p, d], fb.at[p, d], fs.at[index], fr.at[index], place))
    for copy in factor_sends:
        copy.start()
    for distance in range(1, 4):
        arrivals(zb2, 1, CHUNKS - 1, distance)
    for copy in factor_sends:
        copy.wait_recv()
    own[1].wait()
    x_wait(1, 0, xn, xn)
    remote(xg.at[xn, 0], xg.at[diagonal, 0], x_sem.at[4], x_recv.at[4], (p, yn, t)).wait_recv()
    remote(xg.at[yn, 1], xg.at[diagonal, 1], x_sem.at[5], x_recv.at[5], (p, xn, t)).wait_recv()

    def scale(index, carry):
        j, m = index // 2, lax.rem(index, 2)
        tile = fb[m, j]
        for e in range(2):
            for piece in range(4):
                spot = (pl.ds(e * half + piece * 16, 16), slice(None))
                block = xg[(j, m) + spot].astype(jnp.float32)
                xs_ref[(m, j) + spot] = (block * tile[e:e + 1, 0:1]).astype(jnp.bfloat16)
        return carry

    lax.fori_loop(0, 8, scale, 0)
    for m in range(2):
        factor_ref[m] = fb[m, d]

    def finish(c, carry):
        for phase, buf in ((0, zb1), (1, zb2)):
            for s in range(4):
                @pl.when(jnp.logical_and(s <= t, t < 3))
                def _():
                    z_send(buf, phase, c, s, 0).wait_send()

                @pl.when(jnp.logical_and(s >= t, t > 0))
                def _():
                    z_send(buf, phase, c, s, 1).wait_send()

                @pl.when(jnp.logical_not(stays(phase, s)))
                def _():
                    spread_remote(phase, c, s).wait_send()

        for step in range(1, 4):
            reduce_send(c, step).wait_send()

        @pl.when(p == 0)
        def _():
            for m in range(2):
                for j in range(4):
                    here = jnp.logical_and(j == d, m == 0)

                    @pl.when(here)
                    def _():
                        spread_local(1, c, d).wait()

                    @pl.when(jnp.logical_not(here))
                    def _():
                        remote(
                            zb2.at[0, c], g_ref.at[m, j, c], as2.at[c, 0], ar2.at[m, j, c], (1, d, t)
                        ).wait_recv()
        return carry

    lax.fori_loop(0, CHUNKS, finish, 0)
    for copy in x_sends + forwards + gram_sends + norm_sends + factor_sends:
        copy.wait_send()

    @pl.when(p == 0)
    def _():
        pair_remote.wait_send()

    @pl.when(p == 1)
    def _():
        w_remote.wait_send()
        pair_local.wait()
        pair_remote.wait_recv()


def fast_local(weights, inputs, cotangent, clip_norm, noise):
    weight_block = weights[0]
    width, column_part = weight_block.shape
    micro_count, example_count, length_count, _ = inputs[0].shape
    tokens = example_count * length_count
    rows = tokens // CHUNKS
    bf16, f32 = jnp.bfloat16, jnp.float32
    x = inputs[0].reshape(micro_count, tokens, width)
    cot = cotangent.reshape(micro_count, CHUNKS, rows, width)
    vmem, dma = pltpu.VMEM, pltpu.SemaphoreType.DMA
    shards = (4, CHUNKS, rows, width)
    clipped, factors, gradients = pl.pallas_call(
        exchange_kernel,
        out_shape=(
            jax.ShapeDtypeStruct((2, 4, tokens, width), bf16),
            jax.ShapeDtypeStruct((2, 8, 128), f32),
            jax.ShapeDtypeStruct((2,) + shards, bf16),
        ),
        in_specs=[
            pl.BlockSpec(memory_space=pltpu.SMEM),
            pl.BlockSpec(memory_space=pl.ANY),
            pl.BlockSpec(memory_space=vmem),
            pl.BlockSpec(memory_space=vmem),
        ],
        out_specs=(
            pl.BlockSpec(memory_space=vmem),
            pl.BlockSpec(memory_space=vmem),
            pl.BlockSpec(memory_space=pl.ANY),
        ),
        scratch_shapes=[
            vmem((width, column_part), bf16),
            vmem((4, 2, tokens, width), bf16),
            vmem(shards, bf16), vmem(shards, bf16), vmem(shards, bf16), vmem(shards, bf16),
            vmem((3,) + shards[1:], bf16),
            vmem((2, tokens, tokens), bf16),
            vmem((2, 4, tokens, tokens), bf16),
            vmem((4, 8, 128), f32),
            vmem((2, 4, 8, 128), f32),
            dma((1,)), dma((1,)), dma((6,)), dma((6,)), dma((4,)),
            dma((2, CHUNKS, 4, 2)), dma((2, CHUNKS, 4)),
            dma((CHUNKS, 4)), dma((CHUNKS, 4)), dma((CHUNKS, 4)), dma((2, 4, CHUNKS)),
            dma((CHUNKS, 3)), dma((CHUNKS, 3)),
            dma((8,)), dma((8,)), dma((3,)), dma((3,)), dma((8,)), dma((8,)),
            dma((1,)), dma((1,)),
        ],
        compiler_params=pltpu.CompilerParams(
            collective_id=0, has_side_effects=True, vmem_limit_bytes=50 * 1024 * 1024
        ),
        name="exchange",
    )(clip_norm, weight_block, x, cot)
    total = lax.dot_general(
        clipped.reshape(-1, width), gradients.reshape(-1, column_part),
        (((0,), (0,)), ((), ())), preferred_element_type=f32,
    )
    bound = clip_norm[0]
    noise_weight = 1.5 / (column_part * 4)
    final_output = (total + noise_weight * bound * noise[0].astype(f32)) / (2 * 4 * example_count)
    return (final_output[None], factors[:, :example_count, 0])


def solution(mesh):
    in_specs = (
        P("pipe", "tensor", "dp"),
        P("pipe", None, "dp", None, "tensor"),
        P(None, "dp", None, "tensor"),
        P(),
        P("pipe", "tensor", "dp"),
    )
    out_specs = (P("pipe", "tensor", "dp"), P(None, "dp"))
    fits = mesh.shape["pipe"] == 2 and mesh.shape["dp"] == 4 and mesh.shape["tensor"] == 4
    program = fast_local if fits else local
    return jax.shard_map(
        program, mesh=mesh, in_specs=in_specs, out_specs=out_specs, check_vma=False)
```
